512 devices in a mesh: dp: 16 (over y, core), mp: 32 (over x, z).
Axes of the slice: x: 4, y: 8, z: 8, core: 2. Of those that a mesh axis runs over, the one named last changes fastest.
Arguments:
- gate_proj: bfloat16 [14336, 8192], P('mp', 'dp'), may hold values from -0.0625 to 0.0625
- up_proj: bfloat16 [14336, 8192], P('mp', 'dp'), may hold values from -0.0625 to 0.0625
- down_proj: bfloat16 [8192, 14336], P('dp', 'mp'), may hold values from -0.25 to 0.25
- partition: int32 [14336], replicated, may hold values from 0 to 14335, as said below
- tokens: bfloat16 [32768, 8192], P('mp', 'dp'), may hold values from -6 to 6
- targets: bfloat16 [32768, 8192], P('mp', 'dp'), may hold values from -3 to 3
- routes: int32 [32768, 1], P('mp'), may hold values from 0 to 31; in each aligned block of 1024 rows (0 to 1023, 1024 to 2047, ...) at most 42 rows name the same one
- combine: bfloat16 [32768], P('mp'), may hold values from 0.19921875 to 1
Outputs:
- down_grad: float32 [32, 448, 8192], P('mp', None, 'dp')
The draws below stay inside these ranges and needn't reach their ends.
Inputs may be any that keep to these rules, and one draw needn't show every extreme that they name: partition is a permutation of 0 to 14335. Of the 448 hidden units n in rows s * 448 to (s + 1) * 448 - 1 of one tensor shard s, at most 21 belong to one expert, and some shard gives exactly 21 to some expert. `routes`: of the 1024 tokens of one index of mp, at most 42 name the same expert, a bound that some block reaches of them.
All inputs are finite; a program needn't handle non-finite values.
Results may differ from the reference program's by a relative error of at most 0.0041.
Values may be sent and summed in bfloat16 or wider, within the bound.
A program may use at most 64 MiB of HBM per device.

```python
import math
import jax
import jax.numpy as jnp
import numpy as np
from jax import lax

D = 8192
EW = 448
TOK_MP = 1024
EXPERTS = 32
FF = 14336
TOKENS = 32768
CAP = 42
N_MP = 32


def draw_partition(key, part):
    key = jax.random.fold_in(key, 11)
    first, second, third = jax.random.split(key, 3)
    average = EW // EXPERTS
    spread = average // 2
    level = jax.random.randint(first, (EXPERTS,), 0, spread + 1)
    level = level.at[0].set(spread).at[EXPERTS - 1].set(0)
    offset = level - jnp.roll(level, 1)
    source = jnp.arange(EXPERTS, dtype=jnp.int32)
    counts = average + offset[(source[None, :] - source[:, None]) % EXPERTS]

    def owners_of(count_row, shard_key):
        listed = jnp.repeat(source, count_row, total_repeat_length=EW)
        return jax.random.permutation(shard_key, listed)
    owner = jax.vmap(owners_of)(counts, jax.random.split(second, EXPERTS)).reshape(FF)
    order = jnp.argsort(owner, stable=True)
    ranked = jnp.zeros((FF,), jnp.int32).at[order].set(jnp.arange(FF, dtype=jnp.int32) - owner[order] * EW)
    shuffles = jax.vmap(lambda place_key: jax.random.permutation(place_key, EW))(jax.random.split(third, EXPERTS))
    return (owner * EW + shuffles[owner, ranked]).astype(jnp.int32)


def steps_of(key, extent, cuts, smallest, high):
    loudness, own = 1.0, jax.random.fold_in(key, 6)
    for axis_at, blocks in cuts:
        draws = jnp.exp(jax.random.uniform(jax.random.fold_in(own, axis_at), (blocks,), jnp.float32, smallest / len(cuts), high / len(cuts)))
        loudness = loudness * jnp.repeat(draws, extent[axis_at] // blocks).reshape([-1 if axis == axis_at else 1 for axis in range(len(extent))])
    return loudness


def assign_block(key, own, number, rows, amount, top, most, slope):
    sequence = jax.random.permutation(key, amount)
    heavy_load, usual = load_shares(amount, rows * top, most, slope, True), load_shares(amount, rows * top, most, slope, False)
    places = jnp.arange(amount)

    def named(tallies, turn):
        used = int((tallies > 0).sum())
        fixed = max(1, used // 4)
        moved = fixed + (places - fixed + turn * (used - fixed)) % max(1, amount - fixed)
        return jnp.zeros((amount,), jnp.int32).at[sequence[jnp.where(places < fixed, places, moved)]].set(jnp.asarray(tallies, jnp.int32))

    tallies = jnp.where(number % 4 == 0, named(heavy_load, number // 4), named(usual, number - number // 4 - 1))
    mixed = jax.random.permutation(jax.random.fold_in(own, 3), amount)
    giver, receiver = mixed[0:amount // 2 * 2:2], mixed[1:amount // 2 * 2:2]
    slack = jnp.minimum(tallies[giver] - 1, most - tallies[receiver]) // 2
    slack = jnp.where((giver == sequence[0]) | (receiver == sequence[0]) | (tallies[receiver] == 0), 0, jnp.maximum(slack, 0))
    moved = jax.random.randint(jax.random.fold_in(own, 4), (amount // 2,), 0, 1 << 20) % (slack + 1)
    tallies = tallies.at[giver].add(-moved).at[receiver].add(moved)
    labels = jnp.searchsorted(jnp.cumsum(tallies), jnp.arange(rows * top), side="right").astype(jnp.int32)
    table = labels.reshape(top, rows).T
    table = table[jax.random.permutation(jax.random.fold_in(own, 1), rows)]
    turn = jax.random.randint(jax.random.fold_in(own, 2), (rows, 1), 0, top)
    return jnp.take_along_axis(table, (jnp.arange(top)[None, :] + turn) % top, axis=1)


def load_shares(count, total, limit, slope, full):
    portions = [(1 << 20) // math.isqrt(standing ** slope) + 1 for standing in range(1, count + 1)]
    largest = limit if full else min(limit, max(-(-total // count), total * portions[0] // sum(portions)))
    least = 1 if total - largest >= count - 1 else 0
    holding, surplus = [largest] + [least] * (count - 1), total - largest - least * (count - 1)
    while surplus > 0:
        free = [i for i in range(1, count) if holding[i] < largest] or [i for i in range(1, count) if holding[i] < limit]
        whole, left = sum([portions[i] for i in free]), surplus
        for i in free:
            extra = min(limit - holding[i], max(1, left * portions[i] // whole), surplus)
            holding[i] = holding[i] + extra
            surplus = surplus - extra
    return np.array(holding)


def bell_draw(rng, dims, scale, most, cuts=(), kind=jnp.bfloat16):
    result = jax.random.normal(rng, dims, jnp.float32) * scale
    if len(cuts) > 0:
        result = steps_of(rng, dims, cuts, -0.22, 0.18) * result
    return jnp.clip(result, min=-most, max=most).astype(kind)


def setup_inputs(seed: int = 0) -> dict:
    seeds = jax.random.split(jax.random.key(seed), 9)
    gate_proj = bell_draw(seeds[0], (FF, D), D ** -0.5, 0.0625, ((0, 32), (1, 16)))
    up_proj = bell_draw(seeds[1], (FF, D), D ** -0.5, 0.0625, ((0, 32), (1, 16)))
    down_proj = bell_draw(seeds[2], (D, FF), EW ** -0.5, 0.25, ((0, 16), (1, 32)))
    partition = draw_partition(jax.random.fold_in(seeds[8], 71), 0)
    tokens = bell_draw(seeds[4], (TOKENS, D), 1.0, 6.0, ((0, 32), (1, 16)))
    targets = bell_draw(seeds[5], (TOKENS, D), 0.5, 3.0, ((0, 32), (1, 16)))
    routes_keys = jax.random.split(jax.random.fold_in(seeds[6], 1), TOKENS // TOK_MP)
    routes_turns = jax.random.permutation(jax.random.fold_in(seeds[6], 3), TOKENS // TOK_MP)
    routes = jax.vmap(lambda own, number: assign_block(jax.random.fold_in(seeds[6], 2), own, number, TOK_MP, EXPERTS, 1, CAP, 1))(routes_keys, routes_turns).reshape((TOKENS, 1))
    combine = jnp.clip(0.19921875 + 0.80078125 * jax.random.uniform(seeds[7], (TOKENS,), jnp.float32) ** steps_of(seeds[7], (TOKENS,), ((0, 32),), -0.2, 0.2), 0.19921875, 1.0).astype(jnp.bfloat16)
    return {"gate_proj": gate_proj, "up_proj": up_proj, "down_proj": down_proj, "partition": partition, "tokens": tokens, "targets": targets, "routes": routes, "combine": combine}


def reference(gate_proj, up_proj, down_proj, partition, tokens, targets, routes, combine):
    slots = N_MP * CAP
    scale = TOK_MP ** -0.5
    inverse = jnp.zeros((FF,), jnp.int32).at[partition].set(jnp.arange(FF, dtype=jnp.int32))
    grouped = routes[:, 0].reshape(N_MP, TOK_MP)
    member = (grouped[:, :, None] == jnp.arange(EXPERTS, dtype=jnp.int32)).astype(jnp.int32)
    ranked = jnp.sum(jnp.cumsum(member, axis=1) * member, axis=2) - 1
    anchor = jnp.arange(TOKENS, dtype=jnp.int32).reshape(N_MP, TOK_MP)
    groups = jnp.broadcast_to(jnp.arange(N_MP, dtype=jnp.int32)[:, None], (N_MP, TOK_MP))
    table = jnp.full((EXPERTS, N_MP, CAP), TOKENS, jnp.int32).at[grouped, groups, ranked].set(anchor)
    padded_rows = jnp.concatenate([tokens, jnp.zeros((1, D), tokens.dtype)], axis=0)
    padded_goal = jnp.concatenate([targets, jnp.zeros((1, D), targets.dtype)], axis=0)
    padded_weight = jnp.concatenate([combine, jnp.zeros((1,), combine.dtype)], axis=0)

    def one_expert(expert):
        picks = lax.dynamic_slice_in_dim(inverse, expert * EW, EW)
        index = lax.dynamic_index_in_dim(table, expert, 0, keepdims=False).reshape(slots)
        rows = padded_rows[index]
        goal = padded_goal[index].astype(jnp.float32)
        weight = padded_weight[index].astype(jnp.float32)[:, None]
        gate_sum = jnp.dot(rows, gate_proj[picks].T, preferred_element_type=jnp.float32)
        up_sum = jnp.dot(rows, up_proj[picks].T, preferred_element_type=jnp.float32)
        hidden = (jax.nn.silu(gate_sum) * up_sum).astype(jnp.bfloat16)
        student = jnp.dot(hidden, down_proj[:, picks].T, preferred_element_type=jnp.float32)
        delta = (weight * (weight * student - goal) * scale).astype(jnp.bfloat16)
        return jnp.dot(hidden.T, delta, preferred_element_type=jnp.float32)

    return lax.map(one_expert, jnp.arange(EXPERTS, dtype=jnp.int32))
```

```python
import functools

import jax
import jax.numpy as jnp
from jax import lax
from jax.experimental import pallas as pl
from jax.experimental.pallas import tpu as pltpu
from jax.sharding import PartitionSpec as P

MESH = pl.DeviceIdType.MESH
BF = jnp.bfloat16
F32 = jnp.float32
I32 = jnp.int32

W_CAP = 21
T_CAP = 42
STRIDE = 64
ROWS = 48
MAIN = 32
TAIL = 16
FOLD = 12
WINDOW = 2


def nn(a, b):
    return jnp.dot(a, b, preferred_element_type=F32)


def nt(a, b):
    return lax.dot_general(a, b, (((1,), (1,)), ((), ())), preferred_element_type=F32)


def tn(a, b):
    return lax.dot_general(a, b, (((0,), (0,)), ((), ())), preferred_element_type=F32)


def onehot(mask):
    return jnp.where(mask, 1.0, 0.0).astype(BF)


def iota(shape, axis):
    return lax.broadcasted_iota(I32, shape, axis)


def body(
    nx, nz, scale,
    gate_ref, up_ref, down_ref, part_ref, tok_ref, goal_ref, route_ref, comb_ref,
    out_ref,
    send_a, send_b, send_c, send_d, recv_a, recv_b, recv_c, recv_d,
    keyr, placer, xa, xb, qa, qc, wt, wd, wcol, grem, pbuf, sibrecv, ringp, ringm, hid, half,
    ssem, rsem, sib_s, sib_r, p_s, p_r, m_s, m_r, h_s, h_r, hs_s, hs_r,
):
    peers = nx * nz
    ny = hid.shape[1]
    chunks = peers // ny
    groups = ny // nx
    units = gate_ref.shape[0]
    cols = gate_ref.shape[1]
    count = tok_ref.shape[0]
    blocks = cols // 128
    folded = send_a.shape[1] - blocks * MAIN
    own_k = nx * (nz - 1)
    hp = ny // 2
    hm = ny - 1 - hp

    mp = lax.axis_index("mp")
    dp = lax.axis_index("dp")
    x, z = mp // nz, mp % nz
    y, c = dp // 2, dp % 2
    sibling = (y * 2 + 1 - c, mp)

    def shift(g):
        a = nz // 2 - 1 - g // 2
        odd = g % 2
        return (1 - odd) * (a + (nz // 2) * ((g + 2) // nz)) + odd * ((nz - a) % nz)

    def dest(g, dx):
        return ((x + dx) % nx) * nz + (z + shift(g)) % nz

    def source(k):
        g, dx = k // nx, k % nx
        return ((x + nx - dx) % nx) * nz + (z + nz - shift(g)) % nz

    def peer_y(dy):
        return ((y + ny + dy) % ny) * 2 + c

    barrier = pltpu.get_barrier_semaphore()

    def greet(k, carry):
        @pl.when(k != own_k)
        def _():
            pl.semaphore_signal(
                barrier, inc=1, device_id=(dp, dest(k // nx, k % nx)), device_id_type=MESH
            )

        return carry

    lax.fori_loop(0, peers, greet, 0)
    for dy in range(1, ny):
        pl.semaphore_signal(barrier, inc=1, device_id=(peer_y(dy), mp), device_id_type=MESH)
    pl.semaphore_signal(barrier, inc=1, device_id=sibling, device_id_type=MESH)

    tri_u = onehot(iota((units, units), 0) <= iota((units, units), 1))
    my_part = part_ref[pl.ds(mp, 1), :]
    my_owner = jnp.floor((my_part.astype(F32) + 0.5) * (1.0 / units)).astype(I32)
    hot = iota((peers, units), 0) == my_owner
    ahead = nn(onehot(hot), tri_u)
    rank = jnp.sum(ahead * jnp.where(hot, 1.0, 0.0), axis=0, keepdims=True) - 1.0
    unit_key = my_owner * STRIDE + rank.astype(I32)

    sends = (send_a, send_b, send_c, send_d)
    recvs = (recv_a, recv_b, recv_c, recv_d)

    def copy_k(kind, k):
        return pltpu.make_async_remote_copy(
            src_ref=sends[kind].at[k],
            dst_ref=recvs[kind].at[k],
            send_sem=ssem.at[kind, k],
            recv_sem=rsem.at[kind, k],
            device_id=(dp, dest(k // nx, k % nx)),
            device_id_type=MESH,
        )

    def chunk_loop(j, step):
        def run(k, carry):
            @pl.when(k != own_k)
            def _():
                step(k)

            return carry

        lax.fori_loop(j * ny, (j + 1) * ny, run, 0)

    def start(kind, j):
        if j < chunks:
            chunk_loop(j, lambda k: copy_k(kind, k).start())

    def sent(kind, j):
        chunk_loop(j, lambda k: copy_k(kind, k).wait_send())

    def arrive(kind, j):
        chunk_loop(j, lambda k: copy_k(kind, k).wait_recv())

    fold_rows = iota((folded, blocks * TAIL), 0)
    fold_cols = iota((folded, blocks * TAIL), 1)
    fold = onehot(
        (fold_cols % TAIL < FOLD) & (fold_rows == (fold_cols // TAIL) * FOLD + fold_cols % TAIL)
    )
    open_rows = iota((blocks * TAIL, folded), 0)
    open_cols = iota((blocks * TAIL, folded), 1)
    unfold = onehot(
        (open_rows % TAIL < FOLD) & (open_cols == (open_rows // TAIL) * FOLD + open_rows % TAIL)
    )

    def column(b):
        return slice(b * 128, (b + 1) * 128)

    def pack(block, send, g):
        tails = []
        for dx in range(nx):
            rows = block[dx * ROWS : (dx + 1) * ROWS]
            for b in range(blocks):
                send[g * nx + dx, b * MAIN : (b + 1) * MAIN, :] = rows[:MAIN, column(b)]
            tails.append(jnp.concatenate([rows[MAIN:, column(b)] for b in range(blocks)], axis=0))
        rest = nn(fold, jnp.concatenate(tails, axis=1)).astype(BF)
        for dx in range(nx):
            send[g * nx + dx, blocks * MAIN :, :] = rest[:, column(dx)]

    def unpack(recv, full, g):
        rest = jnp.concatenate([recv[g * nx + dx, blocks * MAIN :, :] for dx in range(nx)], axis=1)
        tails = nn(unfold, rest).astype(BF)
        for dx in range(nx):
            k = g * nx + dx
            for b in range(blocks):
                full[k, :MAIN, column(b)] = recv[k, b * MAIN : (b + 1) * MAIN, :]
                full[k, MAIN:, column(b)] = tails[b * TAIL : (b + 1) * TAIL, column(dx)]

    def pick_of(key, g, rows, add):
        parts = []
        for dx in range(nx):
            want = iota((rows, key.shape[1]), 0) + (dest(g, dx) * STRIDE + add)
            parts.append(onehot(key == want))
        return jnp.concatenate(parts, axis=0)

    def make_a(g, carry):
        block = nn(pick_of(unit_key, g, ROWS, 0), gate_ref[...])
        block += nn(pick_of(unit_key, g, ROWS, -W_CAP), up_ref[...])
        pack(block.astype(BF), send_a, g)
        return carry

    for j in range(chunks):
        lax.fori_loop(j * groups, (j + 1) * groups, make_a, 0)
        if j == 0:
            pl.semaphore_wait(barrier, peers - 1 + ny)
        start(0, j)

    tri_t = onehot(iota((128, 128), 0) <= iota((128, 128), 1))
    before = jnp.zeros((peers, 1), F32)
    keys = []
    for b in range(count // 128):
        chosen = route_ref[:, column(b)]
        hot = iota((peers, 128), 0) == chosen
        ahead = nn(onehot(hot), tri_t) + before
        rank = jnp.sum(ahead * jnp.where(hot, 1.0, 0.0), axis=0, keepdims=True) - 1.0
        keys.append(chosen * STRIDE + rank.astype(I32))
        before = ahead[:, 127:128]
    token_key = jnp.concatenate(keys, axis=1)

    comb_rows = comb_ref[...].astype(F32)
    comb = jnp.concatenate([comb_rows[b : b + 1] for b in range(count // 128)], axis=1)
    comb = jnp.broadcast_to(comb, (16, count)).astype(BF)

    def make_b(g, carry):
        pack(nn(pick_of(token_key, g, ROWS, 0), tok_ref[...]).astype(BF), send_b, g)
        return carry

    def make_cd(g, carry):
        main = nn(pick_of(token_key, g, MAIN, 0), goal_ref[...]).astype(BF)
        late = pick_of(token_key, g, MAIN, MAIN - W_CAP)
        low = iota(late.shape, 0) % MAIN >= W_CAP
        late = jnp.where(low, late.astype(F32), 0.0).astype(BF)
        block = nn(late, goal_ref[...]) + nn(pick_of(unit_key, g, MAIN, 0), down_ref[...])
        weights = nt(comb, pick_of(token_key, g, STRIDE, 0))
        for dx in range(nx):
            k = g * nx + dx
            rows = block[dx * MAIN : (dx + 1) * MAIN]
            lanes = weights[0:1, column(dx // 2)]
            first = jnp.where(iota((MAIN, 128), 0) == MAIN - 1, lanes, rows[:, :128])
            send_c[k, :, :128] = first.astype(BF)
            send_c[k, :, 128:] = rows[:, 128:].astype(BF)
            send_d[k] = main[dx * MAIN : (dx + 1) * MAIN]
        return carry

    lax.fori_loop(0, nz, make_b, 0)
    lax.fori_loop(0, nz, make_cd, 0)
    for send, recv in zip(sends, recvs):
        recv[own_k] = send[own_k]

    part = part_ref[...]
    owner = jnp.floor((part.astype(F32) + 0.5) * (1.0 / units)).astype(I32)
    mine = owner == mp
    ahead = nn(onehot(mine), tri_u)
    keyr[...] = jnp.where(mine, ahead.astype(I32) - 1, -1000)
    placer[...] = jnp.where(mine, part - owner * units + 1, 0).astype(F32)

    def landing(k, rows):
        s = source(k)
        row = iota((rows, 1), 0)
        second = (row >= W_CAP).astype(I32) if rows == ROWS else jnp.zeros((rows, 1), I32)
        match = keyr[pl.ds(s, 1), :] == row - second * W_CAP
        found = jnp.sum(jnp.where(match, placer[pl.ds(s, 1), :], 0.0), axis=1, keepdims=True)
        return jnp.where(found > 0.0, found.astype(I32) - 1 + second * units, -1)

    def place_a(k, carry):
        qa[k] = onehot(landing(k, ROWS) == iota((ROWS, 2 * units), 1))
        return carry

    def place_c(k, carry):
        qc[k] = onehot(landing(k, MAIN) == iota((MAIN, units), 1))
        return carry

    lax.fori_loop(0, peers, place_a, 0)
    lax.fori_loop(0, peers, place_c, 0)

    for j in range(chunks):
        sent(0, j)
        if j < WINDOW:
            start(1, j)
    for j in range(chunks):
        arrive(0, j)

    def open_a(g, carry):
        unpack(recv_a, xa, g)
        return carry

    lax.fori_loop(0, nz, open_a, 0)
    wt[...] = tn(
        xa[...].reshape(peers * ROWS, cols), qa[...].reshape(peers * ROWS, 2 * units)
    ).astype(BF)

    def on_owner(stage):
        def run(j):
            @pl.when(c == j % 2)
            def _():
                stage(j)

        return run

    def remote(src, dst, send, recv, target):
        return pltpu.make_async_remote_copy(
            src_ref=src, dst_ref=dst, send_sem=send, recv_sem=recv,
            device_id=target, device_id_type=MESH,
        )

    def sib_copy(j):
        return remote(pbuf.at[j], sibrecv.at[j // 2], sib_s.at[j], sib_r.at[j], sibling)

    def plus_copy(j, s):
        src = pbuf.at[j, (y + hp) % ny] if s == 0 else ringp.at[j // 2, s - 1]
        return remote(src, ringp.at[j // 2, s], p_s.at[j, s], p_r.at[j, s], (peer_y(1), mp))

    def minus_copy(j, s):
        src = pbuf.at[j, (y + ny - hm) % ny] if s == 0 else ringm.at[j // 2, s - 1]
        return remote(src, ringm.at[j // 2, s], m_s.at[j, s], m_r.at[j, s], (peer_y(-1), mp))

    def h_copy(j, dy):
        return remote(hid.at[j, y], hid.at[j, y], h_s.at[j, dy], h_r.at[j, dy], (peer_y(dy), mp))

    def h_arrival(j, dy):
        src = (y + ny - dy) % ny
        return remote(hid.at[j, src], hid.at[j, src], h_s.at[j, dy], h_r.at[j, dy], (peer_y(dy), mp))

    def hs_copy(j):
        return remote(hid.at[j], hid.at[j], hs_s.at[j], hs_r.at[j], sibling)

    def partial(j):
        arrive(1, j)

        def open_b(g, carry):
            unpack(recv_b, xb, g)
            return carry

        lax.fori_loop(j * groups, (j + 1) * groups, open_b, 0)
        rows = xb[j * ny : (j + 1) * ny].reshape(ny * ROWS, cols)
        pbuf[j] = nn(rows, wt[...]).reshape(ny, ROWS, 2 * units)

        @pl.when(c != j % 2)
        def _():
            sib_copy(j).start()

    @on_owner
    def ring_first(j):
        sib_copy(j).wait_recv()
        pbuf[j] += sibrecv[j // 2]
        plus_copy(j, 0).start()
        if hm > 0:
            minus_copy(j, 0).start()

    def ring_step(s):
        @on_owner
        def run(j):
            if s < hp:
                plus_copy(j, s - 1).wait_recv()
                ringp[j // 2, s - 1] += pbuf[j, (y + hp - s) % ny]
                plus_copy(j, s).start()
            if s < hm:
                minus_copy(j, s - 1).wait_recv()
                ringm[j // 2, s - 1] += pbuf[j, (y + ny - hm + s) % ny]
                minus_copy(j, s).start()

        return run

    @on_owner
    def combine(j):
        plus_copy(j, hp - 1).wait_recv()
        total = pbuf[j, y] + ringp[j // 2, hp - 1]
        if hm > 0:
            minus_copy(j, hm - 1).wait_recv()
            total += ringm[j // 2, hm - 1]
        gate = total[:, :units]
        value = gate / (1.0 + jnp.exp(-gate)) * total[:, units:]
        hid[j, y] = value.astype(BF)
        for dy in range(1, ny):
            h_copy(j, dy).start()

    @on_owner
    def share(j):
        for dy in range(1, ny):
            h_arrival(j, dy).wait_recv()
        hs_copy(j).start()

    pick_late = onehot(
        (iota((TAIL, MAIN), 1) == iota((TAIL, MAIN), 0) + W_CAP)
        & (iota((TAIL, MAIN), 0) < T_CAP - MAIN)
    )

    def open_c(j):
        arrive(2, j)

        def run(k, carry):
            grem[k] = nn(pick_late, recv_c[k]).astype(BF)
            last = recv_c[k, MAIN - 16 :, 0:128].astype(F32)[15:16]
            lane = iota((ROWS, 128), 1) - (k % nx % 2) * STRIDE
            eye = lane == iota((ROWS, 128), 0)
            wcol[k] = jnp.sum(jnp.where(eye, last, 0.0), axis=1, keepdims=True)
            return carry

        lax.fori_loop(j * ny, (j + 1) * ny, run, 0)

    def close_c():
        wd[...] = tn(
            qc[...].reshape(peers * MAIN, units), recv_c[...].reshape(peers * MAIN, cols)
        ).astype(BF)

    def student(j):
        @pl.when(c != j % 2)
        def _():
            hs_copy(j).wait_recv()

        weight = wcol[j * ny : (j + 1) * ny].reshape(ny * ROWS, 1)
        half[j] = weight * nn(hid[j].reshape(ny * ROWS, units), wd[...])

    def finish(j):
        arrive(3, j)
        goal = jnp.concatenate(
            [recv_d[j * ny : (j + 1) * ny], grem[j * ny : (j + 1) * ny]], axis=1
        ).reshape(ny * ROWS, cols)
        weight = wcol[j * ny : (j + 1) * ny].reshape(ny * ROWS, 1)
        delta = (weight * (half[j] - goal.astype(F32)) * scale).astype(BF)
        gradient = tn(hid[j].reshape(ny * ROWS, units), delta)
        if j == 0:
            out_ref[...] = gradient
        else:
            out_ref[...] += gradient

    ring_steps = [ring_step(s) for s in range(1, max(hp, hm))]
    stages = [partial, ring_first] + ring_steps + [combine, share]
    followers = {}

    def follow(kind, j, *starts):
        followers[len(followers)] = (kind, j, starts)

    for j in range(chunks):
        if j + WINDOW < chunks:
            follow(1, j, (1, j + WINDOW))
        elif j + 1 < chunks:
            follow(1, j, (2, 0), (2, 1))
        else:
            rest = [(2, i) for i in range(2 if chunks > 1 else 0, chunks)]
            follow(1, j, *rest, (3, 0))
    for j in range(chunks):
        follow(2, j, (3, j + 1))
    for t in range(max(chunks + len(stages) - 1, len(followers))):
        for at in reversed(range(1, len(stages))):
            if 0 <= t - at < chunks:
                stages[at](t - at)
        if t < chunks:
            partial(t)
        if t in followers:
            kind, j, starts = followers[t]
            sent(kind, j)
            for later in starts:
                start(*later)
    for j in range(chunks):
        open_c(j)
    close_c()
    for j in range(chunks):
        student(j)
    for j in range(chunks):
        finish(j)

    for j in range(chunks):
        sent(3, j)
    for j in range(chunks):
        @pl.when(c == j % 2)
        def _():
            for s in range(hp):
                plus_copy(j, s).wait_send()
            for s in range(hm):
                minus_copy(j, s).wait_send()
            for dy in range(1, ny):
                h_copy(j, dy).wait_send()
            hs_copy(j).wait_send()

        @pl.when(c != j % 2)
        def _():
            sib_copy(j).wait_send()


def build(mesh, nx, nz):
    peers = mesh.shape["mp"]
    ny = mesh.shape["dp"] // 2
    chunks = peers // ny
    slots = (chunks + 1) // 2
    hp = ny // 2
    hm = max(1, ny - 1 - hp)

    def local(gate_proj, up_proj, down_proj, partition, tokens, targets, routes, combine):
        units, cols = gate_proj.shape
        count = tokens.shape[0]
        blocks = cols // 128
        packed = blocks * MAIN + -(-blocks * FOLD // 16) * 16
        vmem = pl.BlockSpec(memory_space=pltpu.VMEM)
        dma = pltpu.SemaphoreType.DMA
        flops = 2 * peers * ROWS * units * cols * 4
        messages = [
            pltpu.VMEM((peers, packed, 128), BF),
            pltpu.VMEM((peers, packed, 128), BF),
            pltpu.VMEM((peers, MAIN, cols), BF),
            pltpu.VMEM((peers, MAIN, cols), BF),
        ]
        gradient = pl.pallas_call(
            functools.partial(body, nx, nz, count ** (-0.5)),
            out_shape=jax.ShapeDtypeStruct((units, cols), F32),
            in_specs=[vmem] * 8,
            out_specs=vmem,
            scratch_shapes=messages + messages + [
                pltpu.VMEM((peers, units), I32),
                pltpu.VMEM((peers, units), F32),
                pltpu.VMEM((peers, ROWS, cols), BF),
                pltpu.VMEM((peers, ROWS, cols), BF),
                pltpu.VMEM((peers, ROWS, 2 * units), BF),
                pltpu.VMEM((peers, MAIN, units), BF),
                pltpu.VMEM((cols, 2 * units), BF),
                pltpu.VMEM((units, cols), BF),
                pltpu.VMEM((peers, ROWS, 1), F32),
                pltpu.VMEM((peers, TAIL, cols), BF),
                pltpu.VMEM((chunks, ny, ROWS, 2 * units), F32),
                pltpu.VMEM((slots, ny, ROWS, 2 * units), F32),
                pltpu.VMEM((slots, hp, ROWS, 2 * units), F32),
                pltpu.VMEM((slots, hm, ROWS, 2 * units), F32),
                pltpu.VMEM((chunks, ny, ROWS, units), BF),
                pltpu.VMEM((chunks, ny * ROWS, cols), F32),
                dma((4, peers)),
                dma((4, peers)),
                dma((chunks,)),
                dma((chunks,)),
                dma((chunks, hp)),
                dma((chunks, hp)),
                dma((chunks, hm)),
                dma((chunks, hm)),
                dma((chunks, ny)),
                dma((chunks, ny)),
                dma((chunks,)),
                dma((chunks,)),
            ],
            compiler_params=pltpu.CompilerParams(
                collective_id=0, has_side_effects=True, vmem_limit_bytes=56 << 20
            ),
            cost_estimate=pl.CostEstimate(
                flops=flops, bytes_accessed=8 << 20, transcendentals=0
            ),
            name="distill",
        )(
            gate_proj,
            up_proj,
            down_proj.T,
            partition.reshape(peers, units),
            tokens,
            targets,
            routes.reshape(1, count),
            combine.reshape(count // 128, 128),
        )
        return gradient[None]

    in_specs = (
        P("mp", "dp"),
        P("mp", "dp"),
        P("dp", "mp"),
        P(),
        P("mp", "dp"),
        P("mp", "dp"),
        P("mp", None),
        P("mp"),
    )
    out_specs = P("mp", None, "dp")
    return jax.shard_map(local, mesh=mesh, in_specs=in_specs, out_specs=out_specs, check_vma=False)


def solution(mesh):
    return build(mesh, 4, mesh.shape["mp"] // 4)
```

```python
import functools

import jax
import jax.numpy as jnp
from jax import lax
from jax.experimental import pallas as pl
from jax.experimental.pallas import tpu as pltpu
from jax.sharding import PartitionSpec as P

MESH = pl.DeviceIdType.MESH
BF = jnp.bfloat16
F32 = jnp.float32
I32 = jnp.int32

W_CAP = 21
T_CAP = 42
STRIDE = 64
ROWS = 48
MAIN = 32
TAIL = 16
FOLD = 12
PIECES = 2


def nn(a, b):
    return jnp.dot(a, b, preferred_element_type=F32)


def nt(a, b):
    return lax.dot_general(a, b, (((1,), (1,)), ((), ())), preferred_element_type=F32)


def tn(a, b):
    return lax.dot_general(a, b, (((0,), (0,)), ((), ())), preferred_element_type=F32)


def onehot(mask):
    return jnp.where(mask, 1.0, 0.0).astype(BF)


def iota(shape, axis):
    return lax.broadcasted_iota(I32, shape, axis)


def body(
    nx, nz, scale,
    gate_ref, up_ref, down_ref, part_ref, tok_ref, goal_ref, route_ref, comb_ref,
    out_ref,
    send_a, send_b, send_c, send_d, recv_a, recv_b, recv_c, recv_d,
    part_rows, keyr, placer, xa, xb, qa, qc, qt, wt, wd, wcol, turned, pbuf, sibrecv, ringp, ringm, hid, half,
    ssem, rsem, sib_s, sib_r, p_s, p_r, m_s, m_r, h_s, h_r, hs_s, hs_r,
):
    peers = nx * nz
    ny = hid.shape[1]
    chunks = peers // ny
    groups = ny // nx
    units = gate_ref.shape[0]
    cols = gate_ref.shape[1]
    count = tok_ref.shape[0]
    blocks = cols // 128
    folded = send_a.shape[1] - blocks * MAIN
    own_k = nx * (nz - 1)
    hp = ny // 2
    hm = ny - 1 - hp

    mp = lax.axis_index("mp")
    dp = lax.axis_index("dp")
    x, z = mp // nz, mp % nz
    y, c = dp // 2, dp % 2
    sibling = (y * 2 + 1 - c, mp)

    def shift(g):
        a = nz // 2 - 1 - g // 2
        odd = g % 2
        return (1 - odd) * (a + (nz // 2) * ((g + 2) // nz)) + odd * ((nz - a) % nz)

    def dest(g, dx):
        return ((x + dx) % nx) * nz + (z + shift(g)) % nz

    def source(k):
        g, dx = k // nx, k % nx
        return ((x + nx - dx) % nx) * nz + (z + nz - shift(g)) % nz

    def peer_y(dy):
        return ((y + ny + dy) % ny) * 2 + c

    barrier = pltpu.get_barrier_semaphore()

    def greet(k, carry):
        @pl.when(k != own_k)
        def _():
            pl.semaphore_signal(
                barrier, inc=1, device_id=(dp, dest(k // nx, k % nx)), device_id_type=MESH
            )

        return carry

    lax.fori_loop(0, peers, greet, 0)
    for dy in range(1, ny):
        pl.semaphore_signal(barrier, inc=1, device_id=(peer_y(dy), mp), device_id_type=MESH)
    pl.semaphore_signal(barrier, inc=1, device_id=sibling, device_id_type=MESH)

    tri_u = onehot(iota((units, units), 0) <= iota((units, units), 1))
    per = 2 * units // 128
    if per * 128 == 2 * units:
        wide = jnp.concatenate(
            [part_ref[pl.ds(i, peers // 2, stride=per), :] for i in range(per)], axis=1
        )
        part_rows[...] = jnp.concatenate([wide[:, :units], wide[:, units:]], axis=0)
    else:
        part_rows[...] = jnp.concatenate([part_ref[h::2, :] for h in range(2)], axis=0)

    def shard_row(s):
        return (s % 2) * (peers // 2) + s // 2

    my_part = part_rows[pl.ds(shard_row(mp), 1), :]
    my_owner = jnp.floor((my_part.astype(F32) + 0.5) * (1.0 / units)).astype(I32)
    hot = iota((peers, units), 0) == my_owner
    ahead = nn(onehot(hot), tri_u)
    rank = jnp.sum(ahead * jnp.where(hot, 1.0, 0.0), axis=0, keepdims=True) - 1.0
    unit_key = my_owner * STRIDE + rank.astype(I32)

    sends = (send_a, send_b, send_c, send_d)
    recvs = (recv_a, recv_b, recv_c, recv_d)

    def copy_k(kind, k):
        return pltpu.make_async_remote_copy(
            src_ref=sends[kind].at[k],
            dst_ref=recvs[kind].at[k],
            send_sem=ssem.at[kind, k],
            recv_sem=rsem.at[kind, k],
            device_id=(dp, dest(k // nx, k % nx)),
            device_id_type=MESH,
        )

    def chunk_loop(j, step):
        def run(k, carry):
            @pl.when(k != own_k)
            def _():
                step(k)

            return carry

        lax.fori_loop(j * ny, (j + 1) * ny, run, 0)

    def start(kind, j):
        if j < chunks:
            chunk_loop(j, lambda k: copy_k(kind, k).start())

    def sent(kind, j):
        chunk_loop(j, lambda k: copy_k(kind, k).wait_send())

    def swap(kind, j, *then):
        def run(at, carry):
            k = j * ny + at

            @pl.when(k != own_k)
            def _():
                copy_k(kind, k).wait_send()

            for later, i in then:

                @pl.when(i * ny + at != own_k)
                def _():
                    copy_k(later, i * ny + at).start()

            return carry

        lax.fori_loop(0, ny, run, 0)

    def arrive(kind, j):
        chunk_loop(j, lambda k: copy_k(kind, k).wait_recv())

    fold_rows = iota((folded, blocks * TAIL), 0)
    fold_cols = iota((folded, blocks * TAIL), 1)
    fold = onehot(
        (fold_cols % TAIL < FOLD) & (fold_rows == (fold_cols // TAIL) * FOLD + fold_cols % TAIL)
    )
    open_rows = iota((blocks * TAIL, folded), 0)
    open_cols = iota((blocks * TAIL, folded), 1)
    unfold = onehot(
        (open_rows % TAIL < FOLD) & (open_cols == (open_rows // TAIL) * FOLD + open_rows % TAIL)
    )

    def column(b):
        return slice(b * 128, (b + 1) * 128)

    def pack(block, send, g):
        tails = []
        for dx in range(nx):
            rows = block[dx * ROWS : (dx + 1) * ROWS]
            for b in range(blocks):
                send[g * nx + dx, b * MAIN : (b + 1) * MAIN, :] = rows[:MAIN, column(b)]
            tails.append(jnp.concatenate([rows[MAIN:, column(b)] for b in range(blocks)], axis=0))
        rest = nn(fold, jnp.concatenate(tails, axis=1)).astype(BF)
        for dx in range(nx):
            send[g * nx + dx, blocks * MAIN :, :] = rest[:, column(dx)]

    def unpack(recv, full, g):
        rest = jnp.concatenate([recv[g * nx + dx, blocks * MAIN :, :] for dx in range(nx)], axis=1)
        tails = nn(unfold, rest).astype(BF)
        for dx in range(nx):
            k = g * nx + dx
            for b in range(blocks):
                full[k, :MAIN, column(b)] = recv[k, b * MAIN : (b + 1) * MAIN, :]
                full[k, MAIN:, column(b)] = tails[b * TAIL : (b + 1) * TAIL, column(dx)]

    def pick_of(key, g, rows, add):
        parts = []
        for dx in range(nx):
            want = iota((rows, key.shape[1]), 0) + (dest(g, dx) * STRIDE + add)
            parts.append(onehot(key == want))
        return jnp.concatenate(parts, axis=0)

    def make_a(g, carry):
        block = nn(pick_of(unit_key, g, ROWS, 0), gate_ref[...])
        block += nn(pick_of(unit_key, g, ROWS, -W_CAP), up_ref[...])
        pack(block.astype(BF), send_a, g)
        return carry

    for j in range(chunks):
        lax.fori_loop(j * groups, (j + 1) * groups, make_a, 0)
        if j == 0:
            pl.semaphore_wait(barrier, peers - 1 + ny)
        start(0, j)

    tri_t = onehot(iota((128, 128), 0) <= iota((128, 128), 1))
    before = jnp.zeros((peers, 1), F32)
    keys = []
    for b in range(count // 128):
        chosen = route_ref[:, column(b)]
        hot = iota((peers, 128), 0) == chosen
        ahead = nn(onehot(hot), tri_t) + before
        rank = jnp.sum(ahead * jnp.where(hot, 1.0, 0.0), axis=0, keepdims=True) - 1.0
        keys.append(chosen * STRIDE + rank.astype(I32))
        before = ahead[:, 127:128]
    token_key = jnp.concatenate(keys, axis=1)

    comb_rows = comb_ref[...].astype(F32)
    comb = jnp.concatenate([comb_rows[b : b + 1] for b in range(count // 128)], axis=1)
    comb = jnp.broadcast_to(comb, (16, count)).astype(BF)

    def make_b(g, carry):
        pack(nn(pick_of(token_key, g, ROWS, 0), tok_ref[...]).astype(BF), send_b, g)
        return carry

    def make_cd(g, carry):
        main = nn(pick_of(token_key, g, MAIN, 0), goal_ref[...]).astype(BF)
        block = nn(pick_of(token_key, g, MAIN, MAIN), goal_ref[...])
        block += nn(pick_of(unit_key, g, MAIN, MAIN - T_CAP), down_ref[...])
        weights = nt(comb, pick_of(token_key, g, STRIDE, 0))
        for dx in range(nx):
            k = g * nx + dx
            rows = block[dx * MAIN : (dx + 1) * MAIN]
            lanes = weights[0:1, column(dx // 2)]
            first = jnp.where(iota((MAIN, 128), 0) == MAIN - 1, lanes, rows[:, :128])
            send_c[k, :, :128] = first.astype(BF)
            send_c[k, :, 128:] = rows[:, 128:].astype(BF)
            send_d[k] = main[dx * MAIN : (dx + 1) * MAIN]
        return carry

    lax.fori_loop(0, nz, make_b, 0)
    lax.fori_loop(0, nz, make_cd, 0)
    for send, recv in zip(sends, recvs):
        recv[own_k] = send[own_k]

    part = part_rows[...]
    owner = jnp.floor((part.astype(F32) + 0.5) * (1.0 / units)).astype(I32)
    mine = owner == mp
    ahead = nn(onehot(mine), tri_u)
    keyr[...] = jnp.where(mine, ahead.astype(I32) - 1, -1000)
    placer[...] = jnp.where(mine, part - owner * units + 1, 0).astype(F32)

    def landing(k, rank, second):
        s = shard_row(source(k))
        match = keyr[pl.ds(s, 1), :] == rank
        found = jnp.sum(jnp.where(match, placer[pl.ds(s, 1), :], 0.0), axis=1, keepdims=True)
        return jnp.where(found > 0.0, found.astype(I32) - 1 + second, -1)

    def place_a(k, carry):
        row = iota((ROWS, 1), 0)
        second = (row >= W_CAP).astype(I32)
        target = landing(k, row - second * W_CAP, second * units)
        qa[k] = onehot(target == iota((ROWS, 2 * units), 1))
        return carry

    def place_c(k, carry):
        row = iota((MAIN, 1), 0) - (T_CAP - MAIN)
        qc[k] = onehot(landing(k, row, 0) == iota((MAIN, units), 1))
        return carry

    lax.fori_loop(0, peers, place_a, 0)
    lax.fori_loop(0, peers, place_c, 0)
    qt[...] = qc[...].reshape(peers * MAIN, units).T

    for j in range(chunks):
        swap(0, j, *[(1, j)] * (j < 1))
    for j in range(chunks):
        arrive(0, j)

    def open_a(g, carry):
        unpack(recv_a, xa, g)
        return carry

    lax.fori_loop(0, nz, open_a, 0)
    wt[...] = tn(
        xa[...].reshape(peers * ROWS, cols), qa[...].reshape(peers * ROWS, 2 * units)
    ).astype(BF)

    if chunks > 1:
        start(1, 1)

    def on_owner(stage):
        def run(j):
            @pl.when(c == j % 2)
            def _():
                stage(j)

        return run

    def remote(src, dst, send, recv, target):
        return pltpu.make_async_remote_copy(
            src_ref=src, dst_ref=dst, send_sem=send, recv_sem=recv,
            device_id=target, device_id_type=MESH,
        )

    order = []
    for s in range(hp):
        order.append(hp - s)
        if s < hm:
            order.append(s - hm)
    order.append(0)

    def sib_copy(j, offset):
        at, block = order.index(offset), (y + ny + offset) % ny
        return remote(
            pbuf.at[j, block], sibrecv.at[j // 2, block], sib_s.at[j, at], sib_r.at[j, at], sibling
        )

    def joined(j, offset):
        sib_copy(j, offset).wait_recv()
        block = (y + ny + offset) % ny
        return pbuf[j, block] + sibrecv[j // 2, block]

    piece = ROWS // PIECES

    def cut(h):
        return pl.ds(h * piece, piece)

    def plus_copy(j, s, h):
        if s == 0:
            src = pbuf.at[j, (y + hp) % ny, cut(h)]
        else:
            src = ringp.at[j // 2, s - 1, cut(h)]
        dst = ringp.at[j // 2, s, cut(h)]
        return remote(src, dst, p_s.at[j, s, h], p_r.at[j, s, h], (peer_y(1), mp))

    def minus_copy(j, s, h):
        if s == 0:
            src = pbuf.at[j, (y + ny - hm) % ny, cut(h)]
        else:
            src = ringm.at[j // 2, s - 1, cut(h)]
        dst = ringm.at[j // 2, s, cut(h)]
        return remote(src, dst, m_s.at[j, s, h], m_r.at[j, s, h], (peer_y(-1), mp))

    far = hp if hp > 1 else 0

    def h_copy(j, dy):
        at, to = (y, dy) if dy != far else ((y + ny - far + 1) % ny, 1)
        return remote(hid.at[j, at], hid.at[j, at], h_s.at[j, dy], h_r.at[j, dy], (peer_y(to), mp))

    def h_arrival(j, dy):
        src = (y + ny - dy) % ny
        return remote(hid.at[j, src], hid.at[j, src], h_s.at[j, dy], h_r.at[j, dy], (peer_y(dy), mp))

    def hs_copy(j):
        return remote(hid.at[j], hid.at[j], hs_s.at[j], hs_r.at[j], sibling)

    def partial(j):
        arrive(1, j)

        def open_b(g, carry):
            unpack(recv_b, xb, g)
            return carry

        lax.fori_loop(j * groups, (j + 1) * groups, open_b, 0)
        rows = xb[j * ny : (j + 1) * ny].reshape(ny * ROWS, cols)
        pbuf[j] = nn(rows, wt[...]).reshape(ny, ROWS, 2 * units)

        @pl.when(c != j % 2)
        def _():
            for offset in order:
                sib_copy(j, offset).start()

    @on_owner
    def ring_first(j):
        pbuf[j, (y + hp) % ny] = joined(j, hp)
        for h in range(PIECES):
            plus_copy(j, 0, h).start()
        if hm > 0:
            pbuf[j, (y + ny - hm) % ny] = joined(j, -hm)
            for h in range(PIECES):
                minus_copy(j, 0, h).start()

    def ring_step(s):
        @on_owner
        def run(j):
            if s < hp:
                block_p = (y + hp - s) % ny
                pbuf[j, block_p] = joined(j, hp - s)
            if s < hm:
                block_m = (y + ny - hm + s) % ny
                pbuf[j, block_m] = joined(j, s - hm)
            for h in range(PIECES):
                if s < hp:
                    plus_copy(j, s - 1, h).wait_recv()
                    ringp[j // 2, s - 1, cut(h)] += pbuf[j, block_p, cut(h)]
                    plus_copy(j, s, h).start()
                if s < hm:
                    minus_copy(j, s - 1, h).wait_recv()
                    ringm[j // 2, s - 1, cut(h)] += pbuf[j, block_m, cut(h)]
                    minus_copy(j, s, h).start()

        return run

    @on_owner
    def combine(j):
        total = joined(j, 0)
        for h in range(PIECES):
            plus_copy(j, hp - 1, h).wait_recv()
            if hm > 0:
                minus_copy(j, hm - 1, h).wait_recv()
        total += ringp[j // 2, hp - 1]
        if hm > 0:
            total += ringm[j // 2, hm - 1]
        gate = total[:, :units]
        value = gate / (1.0 + jnp.exp(-gate)) * total[:, units:]
        hid[j, y] = value.astype(BF)
        for dy in range(1, ny):
            if dy != far:
                h_copy(j, dy).start()

    @on_owner
    def share(j):
        if far:
            h_arrival(j, far - 1).wait_recv()
            h_copy(j, far).start()
        for dy in range(1, ny):
            if dy != far - 1:
                h_arrival(j, dy).wait_recv()
        hs_copy(j).start()

    def open_c(j):
        arrive(2, j)

        def run(k, carry):
            last = recv_c[k, MAIN - 16 :, 0:128].astype(F32)[15:16]
            lane = iota((ROWS, 128), 1) - (k % nx % 2) * STRIDE
            eye = lane == iota((ROWS, 128), 0)
            wcol[k] = jnp.sum(jnp.where(eye, last, 0.0), axis=1, keepdims=True)
            return carry

        lax.fori_loop(j * ny, (j + 1) * ny, run, 0)

    def close_c():
        wd[...] = nn(qt[...], recv_c[...].reshape(peers * MAIN, cols)).astype(BF)

    def student(j):
        @pl.when(c != j % 2)
        def _():
            hs_copy(j).wait_recv()

        weight = wcol[j * ny : (j + 1) * ny].reshape(ny * ROWS, 1)
        hidden = hid[j].reshape(ny * ROWS, units)
        half[j] = weight * nn(hidden, wd[...])
        turned[j] = hidden.T

    def finish(j):
        arrive(3, j)
        goal = jnp.concatenate(
            [recv_d[j * ny : (j + 1) * ny], recv_c[j * ny : (j + 1) * ny, :TAIL]], axis=1
        ).reshape(ny * ROWS, cols)
        weight = wcol[j * ny : (j + 1) * ny].reshape(ny * ROWS, 1)
        delta = (weight * (half[j] - goal.astype(F32)) * scale).astype(BF)
        gradient = nn(turned[j], delta)
        if j == 0:
            out_ref[...] = gradient
        else:
            out_ref[...] += gradient

    ring_steps = [ring_step(s) for s in range(1, max(hp, hm))]
    queue = [(kind, j) for kind in (1, 2, 3) for j in range(chunks)]
    queue = queue[2 if chunks > 1 else 1 :]
    pace = (1, 1, 2, 3, 2, 1)

    def at(stages, j):
        if 0 <= j < chunks:
            for stage in stages:
                stage(j)

    for t in range(chunks + 2):
        at([partial], t)
        for _ in range(pace[min(t, len(pace) - 1)]):
            if queue:
                start(*queue.pop(0))
        at([ring_first], t)
        at([combine], t - 2)
        at([share], t - 3)
        at(ring_steps[1:2], t - 1)
        at(ring_steps[:1], t)
        at(ring_steps[2:], t - 1)
    while queue:
        start(*queue.pop(0))
    for j in range(chunks):
        open_c(j)
    close_c()
    at([share], chunks - 1)
    for j in range(max(1, chunks - 1)):
        student(j)
    finish(0)
    if chunks > 1:
        student(chunks - 1)
    for j in range(1, chunks):
        finish(j)

    for j in range(chunks):
        for kind in (1, 2, 3):
            sent(kind, j)
    for j in range(chunks):
        @pl.when(c == j % 2)
        def _():
            for h in range(PIECES):
                for s in range(hp):
                    plus_copy(j, s, h).wait_send()
                for s in range(hm):
                    minus_copy(j, s, h).wait_send()
            for dy in range(1, ny):
                h_copy(j, dy).wait_send()
            hs_copy(j).wait_send()

        @pl.when(c != j % 2)
        def _():
            for offset in order:
                sib_copy(j, offset).wait_send()


def build(mesh, nx, nz):
    peers = mesh.shape["mp"]
    ny = mesh.shape["dp"] // 2
    chunks = peers // ny
    slots = (chunks + 1) // 2
    hp = ny // 2
    hm = max(1, ny - 1 - hp)

    def local(gate_proj, up_proj, down_proj, partition, tokens, targets, routes, combine):
        units, cols = gate_proj.shape
        count = tokens.shape[0]
        blocks = cols // 128
        packed = blocks * MAIN + -(-blocks * FOLD // 16) * 16
        whole = 2 * units % 128 == 0
        part_shape = (partition.size // 128, 128) if whole else (peers, units)
        vmem = pl.BlockSpec(memory_space=pltpu.VMEM)
        dma = pltpu.SemaphoreType.DMA
        flops = 2 * peers * ROWS * units * cols * 4
        messages = [
            pltpu.VMEM((peers, packed, 128), BF),
            pltpu.VMEM((peers, packed, 128), BF),
            pltpu.VMEM((peers, MAIN, cols), BF),
            pltpu.VMEM((peers, MAIN, cols), BF),
        ]
        gradient = pl.pallas_call(
            functools.partial(body, nx, nz, count ** (-0.5)),
            out_shape=jax.ShapeDtypeStruct((units, cols), F32),
            in_specs=[vmem] * 8,
            out_specs=vmem,
            scratch_shapes=messages + messages + [
                pltpu.VMEM((peers, units), I32),
                pltpu.VMEM((peers, units), I32),
                pltpu.VMEM((peers, units), F32),
                pltpu.VMEM((peers, ROWS, cols), BF),
                pltpu.VMEM((peers, ROWS, cols), BF),
                pltpu.VMEM((peers, ROWS, 2 * units), BF),
                pltpu.VMEM((peers, MAIN, units), BF),
                pltpu.VMEM((units, peers * MAIN), BF),
                pltpu.VMEM((cols, 2 * units), BF),
                pltpu.VMEM((units, cols), BF),
                pltpu.VMEM((peers, ROWS, 1), F32),
                pltpu.VMEM((chunks, units, ny * ROWS), BF),
                pltpu.VMEM((chunks, ny, ROWS, 2 * units), F32),
                pltpu.VMEM((slots, ny, ROWS, 2 * units), F32),
                pltpu.VMEM((slots, hp, ROWS, 2 * units), F32),
                pltpu.VMEM((slots, hm, ROWS, 2 * units), F32),
                pltpu.VMEM((chunks, ny, ROWS, units), BF),
                pltpu.VMEM((chunks, ny * ROWS, cols), F32),
                dma((4, peers)),
                dma((4, peers)),
                dma((chunks, ny)),
                dma((chunks, ny)),
                dma((chunks, hp, PIECES)),
                dma((chunks, hp, PIECES)),
                dma((chunks, hm, PIECES)),
                dma((chunks, hm, PIECES)),
                dma((chunks, ny)),
                dma((chunks, ny)),
                dma((chunks,)),
                dma((chunks,)),
            ],
            compiler_params=pltpu.CompilerParams(
                collective_id=0, has_side_effects=True, vmem_limit_bytes=56 << 20
            ),
            cost_estimate=pl.CostEstimate(
                flops=flops, bytes_accessed=8 << 20, transcendentals=0
            ),
            name="distill",
        )(
            gate_proj,
            up_proj,
            down_proj.T,
            partition.reshape(part_shape),
            tokens,
            targets,
            routes.reshape(1, count),
            combine.reshape(count // 128, 128),
        )
        return gradient[None]

    in_specs = (
        P("mp", "dp"),
        P("mp", "dp"),
        P("dp", "mp"),
        P(),
        P("mp", "dp"),
        P("mp", "dp"),
        P("mp", None),
        P("mp"),
    )
    out_specs = P("mp", None, "dp")
    return jax.shard_map(local, mesh=mesh, in_specs=in_specs, out_specs=out_specs, check_vma=False)


def solution(mesh):
    return build(mesh, 4, mesh.shape["mp"] // 4)
```

```python
import functools

import jax
import jax.numpy as jnp
from jax import lax
from jax.experimental import pallas as pl
from jax.experimental.pallas import tpu as pltpu
from jax.sharding import PartitionSpec as P

MESH = pl.DeviceIdType.MESH
BF = jnp.bfloat16
F32 = jnp.float32
I32 = jnp.int32

W_CAP = 21
T_CAP = 42
STRIDE = 64
ROWS = 48
MAIN = 32
TAIL = 16
FOLD = 12
PIECES = 2


def nn(a, b):
    return jnp.dot(a, b, preferred_element_type=F32)


def nt(a, b):
    return lax.dot_general(a, b, (((1,), (1,)), ((), ())), preferred_element_type=F32)


def tn(a, b):
    return lax.dot_general(a, b, (((0,), (0,)), ((), ())), preferred_element_type=F32)


def onehot(mask):
    return jnp.where(mask, 1.0, 0.0).astype(BF)


def iota(shape, axis):
    return lax.broadcasted_iota(I32, shape, axis)


def body(
    nx, nz, scale,
    gate_ref, up_ref, down_hbm, part_ref, tok_hbm, goal_hbm, route_ref, comb_ref,
    out_ref, down_ref, tok_ref, goal_ref, load_sem,
    send_a, send_b, send_c, send_d, recv_a, recv_b, recv_c, recv_d,
    part_rows, keyr, placer, xa, xb, qa, qc, qt, wt, wd, wcol, turned, pbuf, sibrecv, ringp, ringm, hid, half,
    ssem, rsem, sib_s, sib_r, p_s, p_r, m_s, m_r, h_s, h_r, hs_s, hs_r,
):
    peers = nx * nz
    ny = hid.shape[1]
    chunks = peers // ny
    groups = ny // nx
    units = gate_ref.shape[0]
    cols = gate_ref.shape[1]
    count = tok_ref.shape[0]
    loads = [
        pltpu.make_async_copy(src, dst, load_sem.at[i])
        for i, (src, dst) in enumerate(
            ((tok_hbm, tok_ref), (goal_hbm, goal_ref), (down_hbm, down_ref))
        )
    ]
    for load in loads:
        load.start()
    blocks = cols // 128
    folded = send_a.shape[1] - blocks * MAIN
    own_k = nx * (nz - 1)
    hp = ny // 2
    hm = ny - 1 - hp

    mp = lax.axis_index("mp")
    dp = lax.axis_index("dp")
    x, z = mp // nz, mp % nz
    y, c = dp // 2, dp % 2
    sibling = (y * 2 + 1 - c, mp)

    def shift(g):
        a = nz // 2 - 1 - g // 2
        odd = g % 2
        return (1 - odd) * (a + (nz // 2) * ((g + 2) // nz)) + odd * ((nz - a) % nz)

    def dest(g, dx):
        return ((x + dx) % nx) * nz + (z + shift(g)) % nz

    def source(k):
        g, dx = k // nx, k % nx
        return ((x + nx - dx) % nx) * nz + (z + nz - shift(g)) % nz

    def peer_y(dy):
        return ((y + ny + dy) % ny) * 2 + c

    barrier = pltpu.get_barrier_semaphore()

    def greet(k, carry):
        @pl.when(k != own_k)
        def _():
            pl.semaphore_signal(
                barrier, inc=1, device_id=(dp, dest(k // nx, k % nx)), device_id_type=MESH
            )

        return carry

    lax.fori_loop(0, peers, greet, 0)
    for dy in range(1, ny):
        pl.semaphore_signal(barrier, inc=1, device_id=(peer_y(dy), mp), device_id_type=MESH)
    pl.semaphore_signal(barrier, inc=1, device_id=sibling, device_id_type=MESH)

    tri_u = onehot(iota((units, units), 0) <= iota((units, units), 1))
    per = 2 * units // 128
    if per * 128 == 2 * units:
        wide = jnp.concatenate(
            [part_ref[pl.ds(i, peers // 2, stride=per), :] for i in range(per)], axis=1
        )
        part_rows[...] = jnp.concatenate([wide[:, :units], wide[:, units:]], axis=0)
    else:
        part_rows[...] = jnp.concatenate([part_ref[h::2, :] for h in range(2)], axis=0)

    def shard_row(s):
        return (s % 2) * (peers // 2) + s // 2

    my_part = part_rows[pl.ds(shard_row(mp), 1), :]
    my_owner = jnp.floor((my_part.astype(F32) + 0.5) * (1.0 / units)).astype(I32)
    hot = iota((peers, units), 0) == my_owner
    ahead = nn(onehot(hot), tri_u)
    rank = jnp.sum(ahead * jnp.where(hot, 1.0, 0.0), axis=0, keepdims=True) - 1.0
    unit_key = my_owner * STRIDE + rank.astype(I32)

    sends = (send_a, send_b, send_c, send_d)
    recvs = (recv_a, recv_b, recv_c, recv_d)

    def copy_k(kind, k):
        return pltpu.make_async_remote_copy(
            src_ref=sends[kind].at[k],
            dst_ref=recvs[kind].at[k],
            send_sem=ssem.at[kind, k],
            recv_sem=rsem.at[kind, k],
            device_id=(dp, dest(k // nx, k % nx)),
            device_id_type=MESH,
        )

    def chunk_loop(j, step):
        def run(k, carry):
            @pl.when(k != own_k)
            def _():
                step(k)

            return carry

        lax.fori_loop(j * ny, (j + 1) * ny, run, 0)

    def start(kind, j):
        if j < chunks:
            chunk_loop(j, lambda k: copy_k(kind, k).start())

    def sent(kind, j):
        chunk_loop(j, lambda k: copy_k(kind, k).wait_send())

    def swap(kind, j, *then):
        def run(at, carry):
            k = j * ny + at

            @pl.when(k != own_k)
            def _():
                copy_k(kind, k).wait_send()

            for later, i in then:

                @pl.when(i * ny + at != own_k)
                def _():
                    copy_k(later, i * ny + at).start()

            return carry

        lax.fori_loop(0, ny, run, 0)

    def arrive(kind, j):
        chunk_loop(j, lambda k: copy_k(kind, k).wait_recv())

    fold_rows = iota((folded, blocks * TAIL), 0)
    fold_cols = iota((folded, blocks * TAIL), 1)
    fold = onehot(
        (fold_cols % TAIL < FOLD) & (fold_rows == (fold_cols // TAIL) * FOLD + fold_cols % TAIL)
    )
    open_rows = iota((blocks * TAIL, folded), 0)
    open_cols = iota((blocks * TAIL, folded), 1)
    unfold = onehot(
        (open_rows % TAIL < FOLD) & (open_cols == (open_rows // TAIL) * FOLD + open_rows % TAIL)
    )

    def column(b):
        return slice(b * 128, (b + 1) * 128)

    def pack(block, send, g):
        tails = []
        for dx in range(nx):
            rows = block[dx * ROWS : (dx + 1) * ROWS]
            for b in range(blocks):
                send[g * nx + dx, b * MAIN : (b + 1) * MAIN, :] = rows[:MAIN, column(b)]
            tails.append(jnp.concatenate([rows[MAIN:, column(b)] for b in range(blocks)], axis=0))
        rest = nn(fold, jnp.concatenate(tails, axis=1)).astype(BF)
        for dx in range(nx):
            send[g * nx + dx, blocks * MAIN :, :] = rest[:, column(dx)]

    def unpack(recv, full, g):
        rest = jnp.concatenate([recv[g * nx + dx, blocks * MAIN :, :] for dx in range(nx)], axis=1)
        tails = nn(unfold, rest).astype(BF)
        for dx in range(nx):
            k = g * nx + dx
            for b in range(blocks):
                full[k, :MAIN, column(b)] = recv[k, b * MAIN : (b + 1) * MAIN, :]
                full[k, MAIN:, column(b)] = tails[b * TAIL : (b + 1) * TAIL, column(dx)]

    def pick_of(key, g, rows, add):
        parts = []
        for dx in range(nx):
            want = iota((rows, key.shape[1]), 0) + (dest(g, dx) * STRIDE + add)
            parts.append(onehot(key == want))
        return jnp.concatenate(parts, axis=0)

    def make_a(g, carry):
        block = nn(pick_of(unit_key, g, ROWS, 0), gate_ref[...])
        block += nn(pick_of(unit_key, g, ROWS, -W_CAP), up_ref[...])
        pack(block.astype(BF), send_a, g)
        return carry

    for j in range(chunks):
        lax.fori_loop(j * groups, (j + 1) * groups, make_a, 0)
        if j == 0:
            pl.semaphore_wait(barrier, peers - 1 + ny)
        start(0, j)

    tri_t = onehot(iota((128, 128), 0) <= iota((128, 128), 1))
    before = jnp.zeros((peers, 1), F32)
    keys = []
    for b in range(count // 128):
        chosen = route_ref[:, column(b)]
        hot = iota((peers, 128), 0) == chosen
        ahead = nn(onehot(hot), tri_t) + before
        rank = jnp.sum(ahead * jnp.where(hot, 1.0, 0.0), axis=0, keepdims=True) - 1.0
        keys.append(chosen * STRIDE + rank.astype(I32))
        before = ahead[:, 127:128]
    token_key = jnp.concatenate(keys, axis=1)

    comb_rows = comb_ref[...].astype(F32)
    comb = jnp.concatenate([comb_rows[b : b + 1] for b in range(count // 128)], axis=1)
    comb = jnp.broadcast_to(comb, (16, count)).astype(BF)

    def make_b(g, carry):
        pack(nn(pick_of(token_key, g, ROWS, 0), tok_ref[...]).astype(BF), send_b, g)
        return carry

    def make_cd(g, carry):
        main = nn(pick_of(token_key, g, MAIN, 0), goal_ref[...]).astype(BF)
        block = nn(pick_of(token_key, g, MAIN, MAIN), goal_ref[...])
        block += nn(pick_of(unit_key, g, MAIN, MAIN - T_CAP), down_ref[...])
        weights = nt(comb, pick_of(token_key, g, STRIDE, 0))
        for dx in range(nx):
            k = g * nx + dx
            rows = block[dx * MAIN : (dx + 1) * MAIN]
            lanes = weights[0:1, column(dx // 2)]
            first = jnp.where(iota((MAIN, 128), 0) == MAIN - 1, lanes, rows[:, :128])
            send_c[k, :, :128] = first.astype(BF)
            send_c[k, :, 128:] = rows[:, 128:].astype(BF)
            send_d[k] = main[dx * MAIN : (dx + 1) * MAIN]
        return carry

    loads[0].wait()
    lax.fori_loop(0, nz, make_b, 0)
    loads[1].wait()
    loads[2].wait()
    lax.fori_loop(0, nz, make_cd, 0)
    for send, recv in zip(sends, recvs):
        recv[own_k] = send[own_k]

    part = part_rows[...]
    owner = jnp.floor((part.astype(F32) + 0.5) * (1.0 / units)).astype(I32)
    mine = owner == mp
    ahead = nn(onehot(mine), tri_u)
    keyr[...] = jnp.where(mine, ahead.astype(I32) - 1, -1000)
    placer[...] = jnp.where(mine, part - owner * units + 1, 0).astype(F32)

    def landing(k, rank, second):
        s = shard_row(source(k))
        match = keyr[pl.ds(s, 1), :] == rank
        found = jnp.sum(jnp.where(match, placer[pl.ds(s, 1), :], 0.0), axis=1, keepdims=True)
        return jnp.where(found > 0.0, found.astype(I32) - 1 + second, -1)

    def place_a(k, carry):
        row = iota((ROWS, 1), 0)
        second = (row >= W_CAP).astype(I32)
        target = landing(k, row - second * W_CAP, second * units)
        qa[k] = onehot(target == iota((ROWS, 2 * units), 1))
        return carry

    def place_c(k, carry):
        row = iota((MAIN, 1), 0) - (T_CAP - MAIN)
        qc[k] = onehot(landing(k, row, 0) == iota((MAIN, units), 1))
        return carry

    lax.fori_loop(0, peers, place_a, 0)
    lax.fori_loop(0, peers, place_c, 0)
    qt[...] = qc[...].reshape(peers * MAIN, units).T

    for j in range(chunks):
        swap(0, j, *[(1, j)] * (j < 1))
    for j in range(chunks):
        arrive(0, j)

    def open_a(g, carry):
        unpack(recv_a, xa, g)
        return carry

    lax.fori_loop(0, nz, open_a, 0)
    wt[...] = tn(
        xa[...].reshape(peers * ROWS, cols), qa[...].reshape(peers * ROWS, 2 * units)
    ).astype(BF)

    if chunks > 1:
        start(1, 1)

    def on_owner(stage):
        def run(j):
            @pl.when(c == j % 2)
            def _():
                stage(j)

        return run

    def remote(src, dst, send, recv, target):
        return pltpu.make_async_remote_copy(
            src_ref=src, dst_ref=dst, send_sem=send, recv_sem=recv,
            device_id=target, device_id_type=MESH,
        )

    order = []
    for s in range(hp):
        order.append(hp - s)
        if s < hm:
            order.append(s - hm)
    order.append(0)

    def sib_copy(j, offset):
        at, block = order.index(offset), (y + ny + offset) % ny
        return remote(
            pbuf.at[j, block], sibrecv.at[j // 2, block], sib_s.at[j, at], sib_r.at[j, at], sibling
        )

    def joined(j, offset):
        sib_copy(j, offset).wait_recv()
        block = (y + ny + offset) % ny
        return pbuf[j, block] + sibrecv[j // 2, block]

    piece = ROWS // PIECES

    def cut(h):
        return pl.ds(h * piece, piece)

    def plus_copy(j, s, h):
        if s == 0:
            src = pbuf.at[j, (y + hp) % ny, cut(h)]
        else:
            src = ringp.at[j // 2, s - 1, cut(h)]
        dst = ringp.at[j // 2, s, cut(h)]
        return remote(src, dst, p_s.at[j, s, h], p_r.at[j, s, h], (peer_y(1), mp))

    def minus_copy(j, s, h):
        if s == 0:
            src = pbuf.at[j, (y + ny - hm) % ny, cut(h)]
        else:
            src = ringm.at[j // 2, s - 1, cut(h)]
        dst = ringm.at[j // 2, s, cut(h)]
        return remote(src, dst, m_s.at[j, s, h], m_r.at[j, s, h], (peer_y(-1), mp))

    far = hp if hp > 1 else 0

    def h_copy(j, dy):
        at, to = (y, dy) if dy != far else ((y + ny - far + 1) % ny, 1)
        return remote(hid.at[j, at], hid.at[j, at], h_s.at[j, dy], h_r.at[j, dy], (peer_y(to), mp))

    def h_arrival(j, dy):
        src = (y + ny - dy) % ny
        return remote(hid.at[j, src], hid.at[j, src], h_s.at[j, dy], h_r.at[j, dy], (peer_y(dy), mp))

    def hs_copy(j):
        return remote(hid.at[j], hid.at[j], hs_s.at[j], hs_r.at[j], sibling)

    def partial(j):
        arrive(1, j)

        def open_b(g, carry):
            unpack(recv_b, xb, g)
            return carry

        lax.fori_loop(j * groups, (j + 1) * groups, open_b, 0)
        rows = xb[j * ny : (j + 1) * ny].reshape(ny * ROWS, cols)
        pbuf[j] = nn(rows, wt[...]).reshape(ny, ROWS, 2 * units)

        @pl.when(c != j % 2)
        def _():
            for offset in order:
                sib_copy(j, offset).start()

    @on_owner
    def ring_first(j):
        pbuf[j, (y + hp) % ny] = joined(j, hp)
        for h in range(PIECES):
            plus_copy(j, 0, h).start()
        if hm > 0:
            pbuf[j, (y + ny - hm) % ny] = joined(j, -hm)
            for h in range(PIECES):
                minus_copy(j, 0, h).start()

    def ring_step(s):
        @on_owner
        def run(j):
            if s < hp:
                block_p = (y + hp - s) % ny
                pbuf[j, block_p] = joined(j, hp - s)
            if s < hm:
                block_m = (y + ny - hm + s) % ny
                pbuf[j, block_m] = joined(j, s - hm)
            for h in range(PIECES):
                if s < hp:
                    plus_copy(j, s - 1, h).wait_recv()
                    ringp[j // 2, s - 1, cut(h)] += pbuf[j, block_p, cut(h)]
                    plus_copy(j, s, h).start()
                if s < hm:
                    minus_copy(j, s - 1, h).wait_recv()
                    ringm[j // 2, s - 1, cut(h)] += pbuf[j, block_m, cut(h)]
                    minus_copy(j, s, h).start()

        return run

    @on_owner
    def combine(j):
        total = joined(j, 0)
        for h in range(PIECES):
            plus_copy(j, hp - 1, h).wait_recv()
            if hm > 0:
                minus_copy(j, hm - 1, h).wait_recv()
        total += ringp[j // 2, hp - 1]
        if hm > 0:
            total += ringm[j // 2, hm - 1]
        gate = total[:, :units]
        value = gate / (1.0 + jnp.exp(-gate)) * total[:, units:]
        hid[j, y] = value.astype(BF)
        for dy in range(1, ny):
            if dy != far:
                h_copy(j, dy).start()

    @on_owner
    def share(j):
        if far:
            h_arrival(j, far - 1).wait_recv()
            h_copy(j, far).start()
        for dy in range(1, ny):
            if dy != far - 1:
                h_arrival(j, dy).wait_recv()
        hs_copy(j).start()

    def open_c(j):
        arrive(2, j)

        def run(k, carry):
            last = recv_c[k, MAIN - 16 :, 0:128].astype(F32)[15:16]
            lane = iota((ROWS, 128), 1) - (k % nx % 2) * STRIDE
            eye = lane == iota((ROWS, 128), 0)
            wcol[k] = jnp.sum(jnp.where(eye, last, 0.0), axis=1, keepdims=True)
            return carry

        lax.fori_loop(j * ny, (j + 1) * ny, run, 0)

    def close_c():
        wd[...] = nn(qt[...], recv_c[...].reshape(peers * MAIN, cols)).astype(BF)

    def student(j):
        @pl.when(c != j % 2)
        def _():
            hs_copy(j).wait_recv()

        weight = wcol[j * ny : (j + 1) * ny].reshape(ny * ROWS, 1)
        hidden = hid[j].reshape(ny * ROWS, units)
        half[j] = weight * nn(hidden, wd[...])
        turned[j] = hidden.T

    def finish(j):
        arrive(3, j)
        goal = jnp.concatenate(
            [recv_d[j * ny : (j + 1) * ny], recv_c[j * ny : (j + 1) * ny, :TAIL]], axis=1
        ).reshape(ny * ROWS, cols)
        weight = wcol[j * ny : (j + 1) * ny].reshape(ny * ROWS, 1)
        delta = (weight * (half[j] - goal.astype(F32)) * scale).astype(BF)
        gradient = nn(turned[j], delta)
        if j == 0:
            out_ref[...] = gradient
        else:
            out_ref[...] += gradient

    ring_steps = [ring_step(s) for s in range(1, max(hp, hm))]
    queue = [(kind, j) for kind in (1, 2, 3) for j in range(chunks)]
    queue = queue[2 if chunks > 1 else 1 :]
    pace = (1, 1, 2, 3, 1, 0)

    def at(stages, j):
        if 0 <= j < chunks:
            for stage in stages:
                stage(j)

    for t in range(chunks + 2):
        at([partial], t)
        for _ in range(pace[min(t, len(pace) - 1)]):
            if queue:
                start(*queue.pop(0))
        at([ring_first], t)
        at([combine], t - 2)
        at([share], t - 3)
        at(ring_steps[1:2], t - 1)
        at(ring_steps[:1], t)
        at(ring_steps[2:], t - 1)
    for j in range(chunks):
        swap(2, j, *queue[:1])
        del queue[:1]
        open_c(j)
    while queue:
        start(*queue.pop(0))
    close_c()
    for j in range(chunks - 2):
        student(j)
    at([share], chunks - 1)
    for j in range(max(0, chunks - 2), chunks):
        student(j)
        if j >= 2:
            finish(j - 2)
    for j in range(max(0, chunks - 2), chunks):
        finish(j)

    for j in range(chunks):
        for kind in (1, 3):
            sent(kind, j)
    for j in range(chunks):
        @pl.when(c == j % 2)
        def _():
            for h in range(PIECES):
                for s in range(hp):
                    plus_copy(j, s, h).wait_send()
                for s in range(hm):
                    minus_copy(j, s, h).wait_send()
            for dy in range(1, ny):
                h_copy(j, dy).wait_send()
            hs_copy(j).wait_send()

        @pl.when(c != j % 2)
        def _():
            for offset in order:
                sib_copy(j, offset).wait_send()


def build(mesh, nx, nz):
    peers = mesh.shape["mp"]
    ny = mesh.shape["dp"] // 2
    chunks = peers // ny
    slots = (chunks + 1) // 2
    hp = ny // 2
    hm = max(1, ny - 1 - hp)

    def local(gate_proj, up_proj, down_proj, partition, tokens, targets, routes, combine):
        units, cols = gate_proj.shape
        count = tokens.shape[0]
        blocks = cols // 128
        packed = blocks * MAIN + -(-blocks * FOLD // 16) * 16
        whole = 2 * units % 128 == 0
        part_shape = (partition.size // 128, 128) if whole else (peers, units)
        vmem = pl.BlockSpec(memory_space=pltpu.VMEM)
        hbm = pl.BlockSpec(memory_space=pl.ANY)
        dma = pltpu.SemaphoreType.DMA
        flops = 2 * peers * ROWS * units * cols * 4
        messages = [
            pltpu.VMEM((peers, packed, 128), BF),
            pltpu.VMEM((peers, packed, 128), BF),
            pltpu.VMEM((peers, MAIN, cols), BF),
            pltpu.VMEM((peers, MAIN, cols), BF),
        ]
        gradient = pl.pallas_call(
            functools.partial(body, nx, nz, count ** (-0.5)),
            out_shape=jax.ShapeDtypeStruct((units, cols), F32),
            in_specs=[vmem, vmem, hbm, vmem, hbm, hbm, vmem, vmem],
            out_specs=vmem,
            scratch_shapes=[
                pltpu.VMEM((units, cols), BF),
                pltpu.VMEM((count, cols), BF),
                pltpu.VMEM((count, cols), BF),
                dma((3,)),
            ] + messages + messages + [
                pltpu.VMEM((peers, units), I32),
                pltpu.VMEM((peers, units), I32),
                pltpu.VMEM((peers, units), F32),
                pltpu.VMEM((peers, ROWS, cols), BF),
                pltpu.VMEM((peers, ROWS, cols), BF),
                pltpu.VMEM((peers, ROWS, 2 * units), BF),
                pltpu.VMEM((peers, MAIN, units), BF),
                pltpu.VMEM((units, peers * MAIN), BF),
                pltpu.VMEM((cols, 2 * units), BF),
                pltpu.VMEM((units, cols), BF),
                pltpu.VMEM((peers, ROWS, 1), F32),
                pltpu.VMEM((chunks, units, ny * ROWS), BF),
                pltpu.VMEM((chunks, ny, ROWS, 2 * units), F32),
                pltpu.VMEM((slots, ny, ROWS, 2 * units), F32),
                pltpu.VMEM((slots, hp, ROWS, 2 * units), F32),
                pltpu.VMEM((slots, hm, ROWS, 2 * units), F32),
                pltpu.VMEM((chunks, ny, ROWS, units), BF),
                pltpu.VMEM((chunks, ny * ROWS, cols), F32),
                dma((4, peers)),
                dma((4, peers)),
                dma((chunks, ny)),
                dma((chunks, ny)),
                dma((chunks, hp, PIECES)),
                dma((chunks, hp, PIECES)),
                dma((chunks, hm, PIECES)),
                dma((chunks, hm, PIECES)),
                dma((chunks, ny)),
                dma((chunks, ny)),
                dma((chunks,)),
                dma((chunks,)),
            ],
            compiler_params=pltpu.CompilerParams(
                collective_id=0, has_side_effects=True, vmem_limit_bytes=56 << 20
            ),
            cost_estimate=pl.CostEstimate(
                flops=flops, bytes_accessed=8 << 20, transcendentals=0
            ),
            name="distill",
        )(
            gate_proj,
            up_proj,
            down_proj.T,
            partition.reshape(part_shape),
            tokens,
            targets,
            routes.reshape(1, count),
            combine.reshape(count // 128, 128),
        )
        return gradient[None]

    in_specs = (
        P("mp", "dp"),
        P("mp", "dp"),
        P("dp", "mp"),
        P(),
        P("mp", "dp"),
        P("mp", "dp"),
        P("mp", None),
        P("mp"),
    )
    out_specs = P("mp", None, "dp")
    return jax.shard_map(local, mesh=mesh, in_specs=in_specs, out_specs=out_specs, check_vma=False)


def solution(mesh):
    return build(mesh, 4, mesh.shape["mp"] // 4)
```
